128 devices in a mesh: seg: 8 (over y, core), freq: 4 (over z), blk: 4 (over x).
Axes of the slice: x: 4, y: 4, z: 4, core: 2. Of those that a mesh axis runs over, the one named last changes fastest.
Arguments:
- samples: bfloat16 [64, 4096, 2048], P(('seg', 'freq'), 'blk'), may hold values from -100 to 100, as said below
- valid_counts: int32 [32], P('blk'), may hold values from 16 to 128, as said below
- channel_mask: int32 [4096], P('blk'), may hold values 0 or 1
- block_pairs: int32 [16, 2], P('blk'), may hold values from 0 to 31, as said below
Outputs:
- stacked: bfloat16 [16, 1024, 2, 128, 128], P('blk', ('seg', 'freq'))
The draws below stay inside these ranges and needn't reach their ends.
Inputs may be any that keep to these rules, and one draw needn't show every extreme that they name: A segment's samples are a scale of its own for each segment and channel times values of order one. `valid_counts`: some block has all 128 channels valid. `block_pairs`: the rows of one index d of blk name a first block in d * 8 to (d + 1) * 8 - 1 and a partner that is 0 to 4 blocks after it; on index 0 one row reaches 4.
All inputs are finite; a program needn't handle non-finite values. No bound on the sum of `channel_mask` on one device may be relied on, other than what follows from the above.
Results may differ from the reference program's by a relative error of at most 0.0064.
Values may be sent and summed in bfloat16 or wider, within the bound.
No kernel may reach another device: no remote copies, remote signals or barrier semaphores. Data moves between devices by JAX's collectives and lax.ppermute only.
A program may use at most 128 MiB of HBM per device.

```python
import math
import jax
import jax.numpy as jnp
from jax import lax

BLOCK = 128
TS = 2048
HB = 4
BLK_DEV = 8
PAIRS_DEV = 4
F = 1024
SEGS = 64
BLOCKS = 32
CH = 4096
PAIRS = 16


def draw_samples(key, part):
    key = jax.random.fold_in(key, 11)
    scale_key, value_key = jax.random.split(key)
    scales = jnp.exp(jax.random.uniform(scale_key, (SEGS, CH, 1), jnp.float32) * math.log(10.0))
    values = jnp.clip(jax.random.normal(value_key, (SEGS, CH, TS), jnp.float32), -6.0, 6.0)
    return (values * scales).astype(jnp.bfloat16)


def draw_valid_counts(key, part):
    key = jax.random.fold_in(key, 22)
    count_key, place_key = jax.random.split(key)
    drawn = jax.random.randint(count_key, (BLOCKS,), BLOCK // 8, BLOCK + 1, jnp.int32)
    chosen = jax.random.randint(place_key, (), 0, BLOCKS, jnp.int32)
    return jnp.where(jnp.arange(BLOCKS, dtype=jnp.int32) == chosen, BLOCK, drawn).astype(jnp.int32)


def draw_block_pairs(key, part):
    key = jax.random.fold_in(key, 33)
    first_key, offset_key = jax.random.split(key)
    rows = jnp.arange(PAIRS, dtype=jnp.int32)
    owner = rows // PAIRS_DEV
    first_block = owner * BLK_DEV + jax.random.randint(first_key, (PAIRS,), 0, BLK_DEV, jnp.int32)
    offsets = jax.random.randint(offset_key, (PAIRS,), 0, HB + 1, jnp.int32)
    forced = rows % PAIRS_DEV == 0
    first_block = jnp.where(forced, owner * BLK_DEV + BLK_DEV - 1, first_block)
    offsets = jnp.where(forced, HB, offsets)
    partner_block = jnp.minimum(first_block + offsets, BLOCKS - 1)
    return jnp.stack([first_block, partner_block], 1).astype(jnp.int32)


def with_ends(entries, own_key, least, high):
    longest = entries.shape.index(max(entries.shape))
    spots = []
    for shift in (0, 1):
        where = [jax.random.randint(jax.random.fold_in(own_key, axis), (), 0, length) for axis, length in enumerate(entries.shape)]
        where[longest] = (where[longest] + shift) % entries.shape[longest]
        spots.append(tuple(where))
    return entries.at[spots[0]].set(least).at[spots[1]].set(high)


def setup_inputs(seed: int = 0) -> dict:
    seeds = jax.random.split(jax.random.key(seed), 5)
    return {
        "samples": draw_samples(jax.random.fold_in(seeds[4], 71), 0),
        "valid_counts": draw_valid_counts(jax.random.fold_in(seeds[4], 71), 0),
        "channel_mask": with_ends((jax.random.randint(seeds[2], (CH,), 0, 8) < 7).astype(jnp.int32), jax.random.fold_in(seeds[2], 1), 0, 1),
        "block_pairs": draw_block_pairs(jax.random.fold_in(seeds[4], 71), 0),
    }


def transform_table(bin_order, samples_len):
    times = jnp.arange(samples_len, dtype=jnp.int32)
    phase = bin_order[:, None] * times[None, :] % samples_len
    angle = phase.astype(jnp.float32) * (2.0 * math.pi / samples_len)
    taper = 0.5 - 0.5 * jnp.cos(times.astype(jnp.float32) * (2.0 * math.pi / samples_len))
    return jnp.stack([taper * jnp.cos(angle), -taper * jnp.sin(angle)], 1).astype(jnp.bfloat16)

def reference(samples, valid_counts, channel_mask, block_pairs):
    table = transform_table(jnp.arange(F, dtype=jnp.int32), TS)
    flat_table = table.reshape(2 * F, TS)
    within = jnp.arange(CH, dtype=jnp.int32) % BLOCK
    limits = jnp.repeat(valid_counts, BLOCK)
    channel_valid = ((within < limits) & (channel_mask == 1)).astype(jnp.float32)

    def whiten_segment(segment):
        spectra = jnp.dot(segment, flat_table.T, preferred_element_type=jnp.float32)
        spectra = jnp.transpose(spectra.reshape(CH, F, 2), (1, 2, 0))
        power_mean = lax.optimization_barrier(jnp.sum(spectra * spectra, axis=(0, 1))) / F
        return (spectra * (lax.rsqrt(power_mean + 1e-06) * channel_valid)).astype(jnp.bfloat16)
    whitened = lax.map(whiten_segment, samples)
    stack_scale = 1.0 / math.sqrt(SEGS)

    def pair_cross(pair_row):
        left_block = lax.dynamic_slice_in_dim(whitened, (pair_row[0] * BLOCK).astype(jnp.int32), BLOCK, 3).astype(jnp.float32)
        right_block = lax.dynamic_slice_in_dim(whitened, (pair_row[1] * BLOCK).astype(jnp.int32), BLOCK, 3).astype(jnp.float32)
        left_real, left_imag = (left_block[:, :, 0], left_block[:, :, 1])
        right_real, right_imag = (right_block[:, :, 0], right_block[:, :, 1])
        cross_real = jnp.einsum('skc,skd->kcd', left_real, right_real) + jnp.einsum('skc,skd->kcd', left_imag, right_imag)
        cross_imag = jnp.einsum('skc,skd->kcd', left_imag, right_real) - jnp.einsum('skc,skd->kcd', left_real, right_imag)
        return (jnp.stack([cross_real, cross_imag], 1) * stack_scale).astype(jnp.bfloat16)
    return lax.map(pair_cross, block_pairs)
```

```python
import math

import jax
import jax.numpy as jnp
import numpy as np
from jax import lax
from jax.experimental import pallas as pl
from jax.experimental.pallas import tpu as pltpu
from jax.sharding import PartitionSpec as P

WIDTH = 128
HB = 4
SIZES = (
    (128, 128), (128, 256), (256, 128), (128, 384), (256, 256), (128, 512), (256, 384), (256, 512), (512, 512),
)
VMEM = 60 * 1024 * 1024


def transform_table(bins, samples_len):
    times = np.arange(samples_len, dtype=np.int64)
    order = np.arange(bins, dtype=np.int64)
    phase = (order[:, None] * times[None, :]) % samples_len
    angle = phase * (2.0 * math.pi / samples_len)
    taper = 0.5 - 0.5 * np.cos(times * (2.0 * math.pi / samples_len))
    table = np.stack([taper * np.cos(angle), -taper * np.sin(angle)], 1)
    return table.reshape(2 * bins, samples_len).astype(np.float32).astype(jnp.bfloat16)


def regroup_matrix():
    out = np.zeros((256, 256), np.float32)
    for src in range(16):
        for row in range(16):
            out[row * 16 + src, src * 16 + row] = 1.0
    return out.astype(jnp.bfloat16)


def spectra_kernel(base, count, steps_in, steps_out, place_ref, samples_ref, table_ref, out_ref, picked, spectra, power):
    step = pl.program_id(0)
    segs, part, samples_len = samples_ref.shape

    @pl.when(step < steps_in)
    def _():
        target = lax.broadcasted_iota(jnp.int32, (count, part), 0) + base
        chosen = (place_ref[...] == target).astype(jnp.bfloat16)
        for s in range(segs):
            rows = jnp.dot(chosen, samples_ref[s], preferred_element_type=jnp.float32).astype(jnp.bfloat16)
            here = pl.ds(s * count, count)

            @pl.when(step == 0)
            def _():
                picked[here, :] = rows

            @pl.when(step > 0)
            def _():
                picked[here, :] = picked[here, :] + rows

    @pl.when(step >= steps_in)
    def _():
        rows = table_ref.shape[0]
        at = step - steps_in
        block = lax.dot_general(table_ref[...], picked[...], (((1,), (1,)), ((), ())), preferred_element_type=jnp.float32)
        spectra[pl.ds(pl.multiple_of(at * rows, rows), rows), :] = block
        squares = jnp.sum(block * block, axis=0, keepdims=True)

        @pl.when(at == 0)
        def _():
            power[...] = squares

        @pl.when(at > 0)
        def _():
            power[...] = power[...] + squares

    @pl.when(step == steps_in + steps_out - 1)
    def _():
        total = spectra.shape[0]
        scale = lax.rsqrt(power[...] / (total // 2) + 1e-06)
        peers, rows, _ = out_ref.shape
        for peer in range(peers):
            out_ref[peer] = (spectra[peer * rows : (peer + 1) * rows, :] * scale).astype(jnp.bfloat16)


def spectra_chunk(samples, table, place, base, count, peers):
    segs, channels, samples_len = samples.shape
    rows_total = table.shape[0]
    part, rows = 256, 512
    steps_in, steps_out = channels // part, rows_total // rows
    body = lambda *refs: spectra_kernel(base, count, steps_in, steps_out, *refs)
    return pl.pallas_call(
        body,
        grid=(steps_in + steps_out,),
        in_specs=[
            pl.BlockSpec((1, part), lambda i: (0, jnp.minimum(i, steps_in - 1))),
            pl.BlockSpec((segs, part, samples_len), lambda i: (0, jnp.minimum(i, steps_in - 1), 0)),
            pl.BlockSpec((rows, samples_len), lambda i: (jnp.maximum(i - steps_in, 0), 0)),
        ],
        out_specs=pl.BlockSpec((peers, rows_total // peers, segs * count), lambda i: (0, 0, 0)),
        out_shape=jax.ShapeDtypeStruct((peers, rows_total // peers, segs * count), jnp.bfloat16),
        scratch_shapes=[
            pltpu.VMEM((segs * count, samples_len), jnp.bfloat16),
            pltpu.VMEM((rows_total, segs * count), jnp.float32),
            pltpu.VMEM((1, segs * count), jnp.float32),
        ],
        compiler_params=pltpu.CompilerParams(vmem_limit_bytes=VMEM),
        cost_estimate=pl.CostEstimate(
            flops=2 * segs * count * samples_len * (rows_total + channels),
            bytes_accessed=2 * (segs * channels * samples_len + rows_total * samples_len),
            transcendentals=0,
        ),
    )(place, samples, table)


def stack_kernel(counts, scale, left_ref, right_ref, next_ref, regroup_ref, xr_ref, xl_ref, zr_ref, out_ref, pick_l, pick_r, pick_n):
    r_count, l_count = counts
    total = r_count + l_count
    pairs, bins, _, width, _ = out_ref.shape
    wide = pairs * width

    @pl.when(pl.program_id(0) == 0)
    def _():
        pick_l[...] = (left_ref[...] == lax.broadcasted_iota(jnp.int32, (wide, total), 1)).astype(jnp.bfloat16)
        pick_r[...] = (right_ref[...] == lax.broadcasted_iota(jnp.int32, (total, wide), 0)).astype(jnp.bfloat16)
        pick_n[...] = (next_ref[...] == lax.broadcasted_iota(jnp.int32, (r_count, wide), 0)).astype(jnp.bfloat16)

    def regrouped(ref, count):
        halves = []
        for h in range(2):
            rows = ref[h * 16 : (h + 1) * 16].reshape(256, 2 * count)
            halves.append(jnp.dot(regroup_ref[...], rows, preferred_element_type=jnp.float32).astype(jnp.bfloat16))
        pieces = []
        for k in range(bins):
            for s in range(2):
                for h in range(2):
                    pieces.append(halves[h][k * 32 : (k + 1) * 32, s * count : (s + 1) * count])
        return jnp.concatenate(pieces, 0)

    xr = regrouped(xr_ref, r_count)
    xl = regrouped(xl_ref, l_count)
    zr = regrouped(zr_ref, r_count)
    right = jnp.dot(xr, pick_r[:r_count], preferred_element_type=jnp.float32)
    right = right + jnp.dot(xl, pick_r[r_count:], preferred_element_type=jnp.float32)
    right = right + jnp.dot(zr, pick_n[...], preferred_element_type=jnp.float32)
    right = right.astype(jnp.bfloat16)
    dims = (((1,), (1,)), ((), ()))
    for k in range(0, bins, 2):
        two = slice(k * 128, (k + 2) * 128)
        left = lax.dot_general(pick_l[:, :r_count], xr[two], dims, preferred_element_type=jnp.float32)
        left = left + lax.dot_general(pick_l[:, r_count:], xl[two], dims, preferred_element_type=jnp.float32)
        left = left.astype(jnp.bfloat16)
        for j in range(2):
            b = right[(k + j) * 128 : (k + j + 1) * 128]
            turned = []
            for g in range(4):
                turned.append(-b[g * 32 + 16 : g * 32 + 32])
                turned.append(b[g * 32 : g * 32 + 16])
            turned = jnp.concatenate(turned, 0)
            for p in range(pairs):
                cols = slice(p * width, (p + 1) * width)
                both = jnp.concatenate([b[:, cols], turned[:, cols]], 1)
                a = left[cols, j * 128 : (j + 1) * 128]
                res = (jnp.dot(a, both, preferred_element_type=jnp.float32) * scale).astype(jnp.bfloat16)
                out_ref[p, k + j, 0] = res[:, :width]
                out_ref[p, k + j, 1] = res[:, width:]


def stacked_products(xr, xl, zr, left_place, right_place, next_place, regroup, pairs, scale):
    peers, rows, r_two = xr.shape
    l_two = xl.shape[2]
    r_count, l_count = r_two // 2, l_two // 2
    total = r_count + l_count
    wide = pairs * WIDTH
    bins = rows // 2
    group = 8
    body = lambda *refs: stack_kernel((r_count, l_count), scale, *refs)
    whole = lambda shape: pl.BlockSpec(shape, lambda g: (0,) * len(shape))
    part = lambda lanes: pl.BlockSpec((peers, 2 * group, lanes), lambda g: (0, g, 0))
    return pl.pallas_call(
        body,
        grid=(bins // group,),
        in_specs=[
            whole((wide, 1)), whole((1, wide)), whole((1, wide)), whole((256, 256)),
            part(r_two), part(l_two), part(r_two),
        ],
        out_specs=pl.BlockSpec((pairs, group, 2, WIDTH, WIDTH), lambda g: (0, g, 0, 0, 0)),
        out_shape=jax.ShapeDtypeStruct((pairs, bins, 2, WIDTH, WIDTH), jnp.bfloat16),
        scratch_shapes=[
            pltpu.VMEM((wide, total), jnp.bfloat16),
            pltpu.VMEM((total, wide), jnp.bfloat16),
            pltpu.VMEM((r_count, wide), jnp.bfloat16),
        ],
        compiler_params=pltpu.CompilerParams(vmem_limit_bytes=VMEM),
        cost_estimate=pl.CostEstimate(
            flops=2 * peers * rows * 2 * wide * (2 * total + r_count),
            bytes_accessed=2 * (peers * rows * (2 * r_two + l_two) + pairs * bins * 2 * WIDTH * WIDTH),
            transcendentals=0,
        ),
    )(left_place, right_place, next_place, regroup, xr, xl, zr)


def shards(samples, valid_counts, channel_mask, block_pairs):
    segs, channels, samples_len = samples.shape
    block_count = valid_counts.shape[0]
    planes = lax.axis_size("blk")
    peers = lax.axis_size("seg") * lax.axis_size("freq")
    pairs = block_pairs.shape[0]
    bins = samples_len // 2
    me = lax.axis_index("blk")
    base_block = me * block_count
    blocks_all = planes * block_count

    table, regroup = lax.optimization_barrier(
        (jnp.asarray(transform_table(bins, samples_len)), jnp.asarray(regroup_matrix()))
    )

    within = jnp.arange(WIDTH, dtype=jnp.int32)[None, :] < valid_counts[:, None]
    valid = (within & (channel_mask.reshape(block_count, WIDTH) == 1)).astype(jnp.int32)
    count_here = jnp.sum(valid, axis=1)

    ids = jnp.arange(blocks_all, dtype=jnp.int32)
    mine = (ids // block_count) == me
    counts_own = jnp.where(mine, jnp.tile(count_here, planes), 0)
    pair_ids = jnp.arange(planes * pairs, dtype=jnp.int32) // pairs
    first_own = jnp.where(pair_ids == me, jnp.tile(block_pairs[:, 0], planes), 0)
    partner_own = jnp.where(pair_ids == me, jnp.tile(block_pairs[:, 1], planes), 0)
    own = jnp.concatenate([counts_own, first_own, partner_own])
    rim_valid = valid[:HB].reshape(1, HB * WIDTH)
    packed = jnp.concatenate([own, rim_valid[0]])
    from_next = lax.ppermute(packed, "blk", [(i, (i - 1) % planes) for i in range(planes)])
    everyone = own + from_next[: own.shape[0]]
    for shift in range(1, planes - 1):
        everyone = everyone + lax.ppermute(own, "blk", [(i, (i + shift) % planes) for i in range(planes)])
    next_valid = from_next[own.shape[0] :].reshape(HB, WIDTH)

    counts = everyone[:blocks_all]
    first = everyone[blocks_all : blocks_all + planes * pairs]
    partner = everyone[blocks_all + planes * pairs :]
    crosses = (first // block_count) != (partner // block_count)
    to_left = jnp.any((partner[None, :] == ids[:, None]) & crosses[None, :], axis=1)
    named = jnp.any((partner[None, :] == ids[:, None]) | (first[None, :] == ids[:, None]), axis=1)
    rim_total = jnp.max(jnp.sum(jnp.where(to_left, counts, 0).reshape(planes, block_count), axis=1))
    all_total = jnp.max(jnp.sum(jnp.where(named, counts, 0).reshape(planes, block_count), axis=1))

    upto = (jnp.arange(WIDTH)[:, None] <= jnp.arange(WIDTH)[None, :]).astype(jnp.bfloat16)

    def ranks(chosen):
        inside = jnp.dot(chosen.astype(jnp.bfloat16), upto, preferred_element_type=jnp.float32).astype(jnp.int32)
        sums = inside[:, -1]
        n = sums.shape[0]
        before = jnp.sum(jnp.where(jnp.arange(n)[None, :] < jnp.arange(n)[:, None], sums[None, :], 0), axis=1)
        return inside - 1 + before[:, None], jnp.sum(sums)

    left_here = lax.dynamic_slice_in_dim(to_left, base_block, block_count)
    named_here = lax.dynamic_slice_in_dim(named, base_block, block_count)
    rim_mask = (valid == 1) & left_here[:, None]
    rest_mask = (valid == 1) & (named_here & ~left_here)[:, None]
    rim_rank, rim_count = ranks(rim_mask)
    rest_rank, _ = ranks(rest_mask)
    place = jnp.where(rim_mask, rim_rank, jnp.where(rest_mask, rest_rank + rim_count, -1))

    padded = jnp.concatenate([to_left, jnp.zeros((HB,), to_left.dtype)])
    left_next = lax.dynamic_slice_in_dim(padded, base_block + block_count, HB)
    next_mask = (next_valid == 1) & left_next[:, None]
    next_rank, _ = ranks(next_mask)
    next_place = jnp.where(next_mask, next_rank, -1)

    first_local = block_pairs[:, 0] - base_block
    partner_local = block_pairs[:, 1] - base_block
    extended = jnp.concatenate([place, jnp.full((HB, WIDTH), -1, jnp.int32)], 0)
    beyond = jnp.concatenate([jnp.full((block_count, WIDTH), -1, jnp.int32), next_place], 0)
    left_place = jnp.take(place, first_local, axis=0).reshape(pairs * WIDTH, 1)
    right_place = jnp.take(extended, partner_local, axis=0).reshape(1, pairs * WIDTH)
    right_next = jnp.take(beyond, partner_local, axis=0).reshape(1, pairs * WIDTH)
    place_row = place.reshape(1, channels)

    scale = 1.0 / math.sqrt(peers * segs)

    def with_sizes(r_count, l_count):
        def run(samples, table, regroup, place_row, left_place, right_place, right_next):
            own_r = spectra_chunk(samples, table, place_row, 0, r_count, peers)
            own_l = spectra_chunk(samples, table, place_row, r_count, l_count, peers)
            xr = lax.all_to_all(own_r, ("seg", "freq"), split_axis=0, concat_axis=0, tiled=True)
            zr = lax.ppermute(xr, "blk", [(i, i - 1) for i in range(1, planes)])
            xl = lax.all_to_all(own_l, ("seg", "freq"), split_axis=0, concat_axis=0, tiled=True)
            return stacked_products(xr, xl, zr, left_place, right_place, right_next, regroup, pairs, scale)

        return run

    fits = jnp.stack([(rim_total <= r) & (all_total <= r + l) for r, l in SIZES[:-1]] + [jnp.bool_(True)])
    branch = jnp.argmax(fits).astype(jnp.int32)
    return lax.switch(
        branch,
        [with_sizes(r, l) for r, l in SIZES],
        samples, table, regroup, place_row, left_place, right_place, right_next,
    )


def solution(mesh):
    placed = (P(("seg", "freq"), "blk", None), P("blk"), P("blk"), P("blk", None))
    return jax.shard_map(
        shards,
        mesh=mesh,
        in_specs=placed,
        out_specs=P("blk", ("seg", "freq"), None, None, None),
        check_vma=False,
    )
```

```python
import math

import jax
import jax.numpy as jnp
import numpy as np
from jax import lax
from jax.experimental import pallas as pl
from jax.experimental.pallas import tpu as pltpu
from jax.sharding import PartitionSpec as P

WIDTH = 128
HB = 4
SIZES = ((128, 320), (192, 320), (256, 384), (320, 448), (512, 512))
VMEM = 60 * 1024 * 1024
NEXT = 1 << 16


def transform_table(bins, samples_len):
    times = np.arange(samples_len, dtype=np.int64)
    order = np.arange(bins, dtype=np.int64)
    phase = (order[:, None] * times[None, :]) % samples_len
    angle = phase * (2.0 * math.pi / samples_len)
    taper = 0.5 - 0.5 * np.cos(times * (2.0 * math.pi / samples_len))
    table = np.stack([taper * np.cos(angle), -taper * np.sin(angle)], 1)
    return table.reshape(2 * bins, samples_len).astype(np.float32).astype(jnp.bfloat16)


def regroup_matrix():
    out = np.zeros((256, 256), np.float32)
    for src in range(16):
        for row in range(16):
            out[row * 16 + src, src * 16 + row] = 1.0
    return out.astype(jnp.bfloat16)


def whole_tiles(count):
    return (count + WIDTH - 1) // WIDTH * WIDTH


def plan_kernel(block_count, me_ref, own_ref, n1_ref, n2_ref, n3_ref, place_ref, where_ref, info_ref):
    refs = (own_ref, n1_ref, n2_ref, n3_ref)
    planes = len(refs)
    me = me_ref[0, 0]
    pairs = where_ref.shape[0] // 2
    firsts = [ref[block_count : block_count + 1, :pairs] for ref in refs]
    partners = [ref[block_count + 1 : block_count + 2, :pairs] for ref in refs]
    flat = lambda x: x.astype(jnp.float32).astype(jnp.bfloat16)
    upto = flat(
        (lax.broadcasted_iota(jnp.int32, (WIDTH, WIDTH), 0) <= lax.broadcasted_iota(jnp.int32, (WIDTH, WIDTH), 1)).astype(jnp.int32)
    )
    row_of = lax.broadcasted_iota(jnp.int32, (block_count, 1), 0)

    def flags(j):
        ids = row_of + lax.rem(me + j, planes) * block_count
        named = jnp.zeros((block_count, 1), jnp.int32)
        rim = jnp.zeros((block_count, 1), jnp.int32)
        for first, partner in zip(firsts, partners):
            hit = partner == ids
            crosses = (first // block_count) != (partner // block_count)
            named = named + jnp.sum((hit | (first == ids)).astype(jnp.int32), axis=1, keepdims=True)
            rim = rim + jnp.sum((hit & crosses).astype(jnp.int32), axis=1, keepdims=True)
        return ids, named > 0, rim > 0

    def ranks(chosen):
        inside = jnp.dot(flat(chosen), upto, preferred_element_type=jnp.float32)
        sums = inside[:, WIDTH - 1 :]
        before = jnp.zeros((block_count, 1), jnp.float32)
        for b in range(block_count - 1):
            before = before + jnp.where(row_of > b, sums[b : b + 1], 0.0)
        return (inside + before).astype(jnp.int32) - 1, jnp.sum(sums, axis=0, keepdims=True).astype(jnp.int32)

    rim_most = jnp.zeros((1, 1), jnp.int32)
    all_list, low_list = [], []
    for j in range(planes):
        ids, named, rim = flags(j)
        valid = refs[j][:block_count]
        counts = jnp.sum(valid, axis=1, keepdims=True)
        total = lambda m: jnp.sum(jnp.where(m, counts, 0), axis=0, keepdims=True)
        rim_most = jnp.maximum(rim_most, total(rim))
        all_list.append(total(named))
        low_list.append(total(named & (row_of < HB)))
        if j == 0:
            own_ids = ids
            rim_mask = jnp.where(rim, valid, 0)
            rest_mask = jnp.where(named & jnp.logical_not(rim), valid, 0)
            rim_rank, rim_count = ranks(rim_mask)
            rest_rank, _ = ranks(rest_mask)
            place = jnp.where(rim_mask > 0, rim_rank, jnp.where(rest_mask > 0, rest_rank + rim_count, -1))
        if j == 1:
            next_ids = ids
            next_mask = jnp.where(rim, valid, 0)
            next_rank, _ = ranks(next_mask)
            next_place = jnp.where(next_mask > 0, next_rank + NEXT, -1)
    branch = jnp.zeros((1, 1), jnp.int32) + (len(SIZES) - 1)
    for n in reversed(range(len(SIZES) - 1)):
        r, l = SIZES[n]
        fits = rim_most <= r
        for everything, low in zip(all_list, low_list):
            fits = fits & (everything - jnp.minimum(low, r) <= l)
        branch = jnp.where(fits, n, branch)
    size = jnp.zeros((1, 1), jnp.int32)
    for n, (r, _) in enumerate(SIZES):
        size = jnp.where(branch == n, r, size)
    behind = jnp.where(row_of >= HB, jnp.maximum(size - low_list[0], 0), 0)
    place = jnp.where(place >= 0, place + behind + whole_tiles(size) - size, -1)
    place_ref[...] = place

    def look(block):
        here = jnp.max(jnp.where(own_ids == block, place, -1), axis=0, keepdims=True)
        beyond = jnp.max(jnp.where(next_ids == block, next_place, -1), axis=0, keepdims=True)
        return jnp.maximum(here, beyond)

    found = [look(firsts[0][:, p : p + 1]) for p in range(pairs)] + [look(partners[0][:, p : p + 1]) for p in range(pairs)]
    found = jnp.concatenate(found, 0)
    where_ref[...] = found
    starts = jnp.min(jnp.where(found >= 0, found, 2 * NEXT), axis=1, keepdims=True)
    starts = jnp.where(starts == 2 * NEXT, 0, starts)
    lanes = lax.broadcasted_iota(jnp.int32, info_ref.shape, 1)
    info_ref[...] = jnp.where(lanes == 0, starts, branch)


def plan(me, own, others, block_count, pairs):
    vmem = pl.BlockSpec(memory_space=pltpu.VMEM)
    return pl.pallas_call(
        lambda *refs: plan_kernel(block_count, *refs),
        in_specs=[pl.BlockSpec(memory_space=pltpu.SMEM)] + [vmem] * 4,
        out_specs=[vmem] * 3,
        out_shape=[
            jax.ShapeDtypeStruct((block_count, WIDTH), jnp.int32),
            jax.ShapeDtypeStruct((2 * pairs, WIDTH), jnp.int32),
            jax.ShapeDtypeStruct((2 * pairs, WIDTH), jnp.int32),
        ],
    )(me, own, *others)


def spectra_kernel(base, count, tile, across, place_ref, samples_ref, table_ref, out_ref, held, table, picked, spectra, power, held_sem, table_sem):
    segs, channels, samples_len = held.shape
    lanes = picked.shape[0]
    pieces = table_sem.shape[0]
    rows = table.shape[0] // pieces

    get = [pltpu.make_async_copy(samples_ref.at[s, :channels, :], held.at[s], held_sem.at[s]) for s in range(segs)]
    for copy in get:
        copy.start()

    def table_copy(n):
        here = pl.ds(pl.multiple_of(n * rows, rows), rows)
        return pltpu.make_async_copy(table_ref.at[here, :], table.at[here, :], table_sem.at[n])

    @pl.loop(0, pieces)
    def _(n):
        table_copy(n).start()

    target = lax.broadcasted_iota(jnp.int32, (count, channels), 0) + base
    chosen = (place_ref[:, :channels] == target).astype(jnp.bfloat16)
    for s in range(segs):
        get[s].wait()

        @pl.loop(0, samples_len // tile)
        def _(n):
            cols = pl.ds(pl.multiple_of(n * tile, tile), tile)
            found = jnp.dot(chosen, held[s, :, cols], preferred_element_type=jnp.float32)
            picked[s * count : (s + 1) * count, cols] = found.astype(jnp.bfloat16)

    power[...] = jnp.zeros(power.shape, jnp.float32)

    @pl.loop(0, pieces)
    def _(n):
        here = pl.ds(pl.multiple_of(n * rows, rows), rows)
        table_copy(n).wait()

        @pl.loop(0, lanes // across)
        def _(m):
            cols = pl.ds(pl.multiple_of(m * across, across), across)
            block = lax.dot_general(
                table[here, :], picked[cols, :], (((1,), (1,)), ((), ())), preferred_element_type=jnp.float32
            )
            spectra[here, cols] = block
            power[:, cols] = power[:, cols] + jnp.sum((block * block).reshape(rows // 8, 8, across), axis=0)

    scale = lax.rsqrt(jnp.sum(power[...], axis=0, keepdims=True) / (table.shape[0] // 2) + 1e-06)
    peers, each, _ = out_ref.shape

    @pl.loop(0, peers)
    def _(peer):
        here = pl.ds(pl.multiple_of(peer * each, each), each)
        out_ref[peer] = (spectra[here, : segs * count] * scale[:, : segs * count]).astype(jnp.bfloat16)


def spectra_chunk(samples, table, place, channels, base, count, peers, urgent):
    segs, _, samples_len = samples.shape
    rows_total = table.shape[0]
    lanes = segs * count
    pieces, tile, across = (4, 512, lanes) if urgent else (4, 256, 256)
    wide = (lanes + across - 1) // across * across
    body = lambda *refs: spectra_kernel(base, count, tile, across, *refs)
    hbm = pl.BlockSpec(memory_space=pl.ANY)
    vmem = pl.BlockSpec(memory_space=pltpu.VMEM)
    return pl.pallas_call(
        body,
        in_specs=[vmem, hbm, hbm],
        out_specs=vmem,
        out_shape=jax.ShapeDtypeStruct((peers, rows_total // peers, lanes), jnp.bfloat16),
        scratch_shapes=[
            pltpu.VMEM((segs, channels, samples_len), jnp.bfloat16),
            pltpu.VMEM((rows_total, samples_len), jnp.bfloat16),
            pltpu.VMEM((wide, samples_len), jnp.bfloat16),
            pltpu.VMEM((rows_total, wide), jnp.float32),
            pltpu.VMEM((8, wide), jnp.float32),
            pltpu.SemaphoreType.DMA((segs,)),
            pltpu.SemaphoreType.DMA((pieces,)),
        ],
        compiler_params=pltpu.CompilerParams(vmem_limit_bytes=VMEM + 7 * 512 * 1024),
        cost_estimate=pl.CostEstimate(
            flops=2 * segs * count * samples_len * (rows_total + channels),
            bytes_accessed=2 * (segs * channels * samples_len + rows_total * samples_len),
            transcendentals=0,
        ),
    )(place, samples, table)


def stack_kernel(counts, scale, info_ref, where_ref, regroup_ref, xr_ref, xl_ref, zr_ref, out_ref, pick_l, pick_r, held):
    r_count, l_count = counts
    own = whole_tiles(r_count) + whole_tiles(l_count)
    pairs, bins, _, width, _ = out_ref.shape
    window = 2 * width
    behind = own + whole_tiles(r_count) - r_count - NEXT

    def start(n):
        first = info_ref[n, 0]
        first = jnp.where(first >= NEXT, first + behind, first)
        return pl.multiple_of((first // width) * width, width)

    @pl.when(pl.program_id(0) == 0)
    def _():
        held[:, held.shape[1] - width :] = jnp.zeros((held.shape[0], width), held.dtype)
        where = where_ref[...]
        where = jnp.where(where >= NEXT, where + behind, where)
        eye = lax.broadcasted_iota(jnp.int32, (width, width), 0) == lax.broadcasted_iota(jnp.int32, (width, width), 1)
        for p in range(pairs):
            pick_l[p] = (where[p : p + 1] == lax.broadcasted_iota(jnp.int32, (window, width), 0) + start(p)).astype(jnp.bfloat16) * jnp.bfloat16(scale)
            row = where[pairs + p : pairs + p + 1]
            pick_r[p] = (row == lax.broadcasted_iota(jnp.int32, (window, width), 0) + start(pairs + p)).astype(jnp.bfloat16)

    chunks = ((xr_ref, r_count, 0, True), (xl_ref, l_count, whole_tiles(r_count), False), (zr_ref, r_count, own, True))
    for ref, count, at, to_end in chunks:
        full = whole_tiles(count)
        for h in range(2):
            rows = ref[h * 16 : (h + 1) * 16].reshape(256, 2 * count)
            rows = jnp.dot(regroup_ref[...], rows, preferred_element_type=jnp.float32)
            by_seg = [rows[:, :full], rows[:, 2 * count - full :]]
            if full != count:
                turn = 0 if to_end else 1
                by_seg[turn] = pltpu.roll(by_seg[turn], WIDTH // 2 if to_end else full - WIDTH // 2, 1)
            for s in range(2):
                part = by_seg[s].astype(jnp.bfloat16)
                for k in range(bins):
                    to = k * 128 + (s * 2 + h) * 32
                    held[to : to + 32, at : at + full] = part[k * 32 : (k + 1) * 32]

    def one_pair(p):
        from_l = held[:, pl.ds(start(p), window)]
        left = jnp.dot(from_l, pick_l[p], preferred_element_type=jnp.float32)
        left = left.astype(jnp.bfloat16)
        from_r = held[:, pl.ds(start(pairs + p), window)]
        right = jnp.dot(from_r, pick_r[p], preferred_element_type=jnp.float32).astype(jnp.bfloat16)
        for k in range(bins):
            b = right[k * 128 : (k + 1) * 128]
            turned = []
            for g in range(4):
                turned.append(-b[g * 32 + 16 : g * 32 + 32])
                turned.append(b[g * 32 : g * 32 + 16])
            both = jnp.concatenate([b, jnp.concatenate(turned, 0)], 1)
            a = left[k * 128 : (k + 1) * 128]
            res = (lax.dot_general(a, both, (((0,), (0,)), ((), ())), preferred_element_type=jnp.float32)).astype(jnp.bfloat16)
            out_ref[p, k, 0] = res[:, :width]
            out_ref[p, k, 1] = res[:, width:]

    pl.loop(0, pairs, unroll=2 if r_count < 512 else 1)(one_pair)


def stacked_products(xr, xl, zr, info, where, regroup, pairs, scale):
    peers, rows, r_two = xr.shape
    l_two = xl.shape[2]
    r_count, l_count = r_two // 2, l_two // 2
    bins = rows // 2
    group = 8
    body = lambda *refs: stack_kernel((r_count, l_count), scale, *refs)
    whole = lambda shape: pl.BlockSpec(shape, lambda g: (0,) * len(shape))
    part = lambda lanes: pl.BlockSpec((peers, 2 * group, lanes), lambda g: (0, g, 0))
    return pl.pallas_call(
        body,
        grid=(bins // group,),
        in_specs=[
            pl.BlockSpec(memory_space=pltpu.SMEM), whole(where.shape), whole((256, 256)),
            part(r_two), part(l_two), part(r_two),
        ],
        out_specs=pl.BlockSpec((pairs, group, 2, WIDTH, WIDTH), lambda g: (0, g, 0, 0, 0)),
        out_shape=jax.ShapeDtypeStruct((pairs, bins, 2, WIDTH, WIDTH), jnp.bfloat16),
        scratch_shapes=[
            pltpu.VMEM((pairs, 2 * WIDTH, WIDTH), jnp.bfloat16),
            pltpu.VMEM((pairs, 2 * WIDTH, WIDTH), jnp.bfloat16),
            pltpu.VMEM((group * 128, 2 * whole_tiles(r_count) + whole_tiles(l_count) + WIDTH), jnp.bfloat16),
        ],
        compiler_params=pltpu.CompilerParams(vmem_limit_bytes=VMEM),
        cost_estimate=pl.CostEstimate(
            flops=2 * peers * rows * 2 * WIDTH * (4 * pairs * WIDTH + 2 * r_two + l_two),
            bytes_accessed=2 * (peers * rows * (2 * r_two + l_two) + pairs * bins * 2 * WIDTH * WIDTH),
            transcendentals=0,
        ),
    )(info, where, regroup, xr, xl, zr)


def shards(samples, valid_counts, channel_mask, block_pairs):
    segs, channels, samples_len = samples.shape
    block_count = valid_counts.shape[0]
    planes = lax.axis_size("blk")
    peers = lax.axis_size("seg") * lax.axis_size("freq")
    pairs = block_pairs.shape[0]
    bins = samples_len // 2

    table, regroup = lax.optimization_barrier(
        (jnp.asarray(transform_table(bins, samples_len)), jnp.asarray(regroup_matrix()))
    )
    within = jnp.arange(WIDTH, dtype=jnp.int32)[None, :] < valid_counts[:, None]
    valid = (within & (channel_mask.reshape(block_count, WIDTH) == 1)).astype(jnp.int32)
    lines = jnp.pad(block_pairs.T, ((0, block_count - 2), (0, WIDTH - pairs)))
    own = jnp.concatenate([valid, lines], 0)
    others = [
        lax.ppermute(own, "blk", [(i, (i - shift) % planes) for i in range(planes)]) for shift in range(1, planes)
    ]
    me = lax.axis_index("blk").astype(jnp.int32).reshape(1, 1)
    place, where, info = plan(me, own, others, block_count, pairs)
    place_row = place.reshape(1, channels)
    scale = 1.0 / math.sqrt(peers * segs)

    def with_sizes(r_count, l_count):
        def run(samples, table, regroup, place_row, where, info):
            own_r = spectra_chunk(samples, table, place_row, HB * WIDTH, whole_tiles(r_count) - r_count, r_count, peers, r_count < 512)
            xr = lax.all_to_all(own_r, ("seg", "freq"), split_axis=0, concat_axis=0, tiled=True)
            own_l = spectra_chunk(samples, table, place_row, channels, whole_tiles(r_count), l_count, peers, False)
            xr, own_l = lax.optimization_barrier((xr, own_l))
            zr = lax.ppermute(xr, "blk", [(i, i - 1) for i in range(1, planes)])
            xl = lax.all_to_all(own_l, ("seg", "freq"), split_axis=0, concat_axis=0, tiled=True)
            return stacked_products(xr, xl, zr, info, where, regroup, pairs, scale)

        return run

    return lax.switch(
        info[0, 1],
        [with_sizes(r, l) for r, l in SIZES],
        samples, table, regroup, place_row, where, info,
    )


def solution(mesh):
    placed = (P(("seg", "freq"), "blk", None), P("blk"), P("blk"), P("blk", None))
    return jax.shard_map(
        shards,
        mesh=mesh,
        in_specs=placed,
        out_specs=P("blk", ("seg", "freq"), None, None, None),
        check_vma=False,
    )
```

```python
import math

import jax
import jax.numpy as jnp
import numpy as np
from jax import lax
from jax.experimental import pallas as pl
from jax.experimental.pallas import tpu as pltpu
from jax.sharding import PartitionSpec as P

WIDTH = 128
HB = 4
SIZES = ((128, 320), (192, 320), (256, 448), (320, 448), (512, 512))
VMEM = 60 * 1024 * 1024
NEXT = 1 << 16


def transform_table(bins, samples_len):
    times = np.arange(samples_len, dtype=np.int64)
    order = np.arange(bins, dtype=np.int64)
    phase = (order[:, None] * times[None, :]) % samples_len
    angle = phase * (2.0 * math.pi / samples_len)
    taper = 0.5 - 0.5 * np.cos(times * (2.0 * math.pi / samples_len))
    table = np.stack([taper * np.cos(angle), -taper * np.sin(angle)], 1)
    return table.reshape(2 * bins, samples_len).astype(np.float32).astype(jnp.bfloat16)


def regroup_matrix():
    out = np.zeros((256, 256), np.float32)
    for src in range(16):
        for row in range(16):
            out[row * 16 + src, src * 16 + row] = 1.0
    return out.astype(jnp.bfloat16)


def whole_tiles(count):
    return (count + WIDTH - 1) // WIDTH * WIDTH


def plan_kernel(block_count, me_ref, own_ref, n1_ref, n2_ref, n3_ref, place_ref, where_ref, info_ref):
    refs = (own_ref, n1_ref, n2_ref, n3_ref)
    planes = len(refs)
    me = me_ref[0, 0]
    pairs = where_ref.shape[0] // 2
    firsts = [ref[block_count : block_count + 1, :pairs] for ref in refs]
    partners = [ref[block_count + 1 : block_count + 2, :pairs] for ref in refs]
    flat = lambda x: x.astype(jnp.float32).astype(jnp.bfloat16)
    upto = flat(
        (lax.broadcasted_iota(jnp.int32, (WIDTH, WIDTH), 0) <= lax.broadcasted_iota(jnp.int32, (WIDTH, WIDTH), 1)).astype(jnp.int32)
    )
    row_of = lax.broadcasted_iota(jnp.int32, (block_count, 1), 0)

    def flags(j):
        ids = row_of + lax.rem(me + j, planes) * block_count
        named = jnp.zeros((block_count, 1), jnp.int32)
        rim = jnp.zeros((block_count, 1), jnp.int32)
        for first, partner in zip(firsts, partners):
            hit = partner == ids
            crosses = (first // block_count) != (partner // block_count)
            named = named + jnp.sum((hit | (first == ids)).astype(jnp.int32), axis=1, keepdims=True)
            rim = rim + jnp.sum((hit & crosses).astype(jnp.int32), axis=1, keepdims=True)
        return ids, named > 0, rim > 0

    def ranks(chosen):
        inside = jnp.dot(flat(chosen), upto, preferred_element_type=jnp.float32)
        sums = inside[:, WIDTH - 1 :]
        before = jnp.zeros((block_count, 1), jnp.float32)
        for b in range(block_count - 1):
            before = before + jnp.where(row_of > b, sums[b : b + 1], 0.0)
        return (inside + before).astype(jnp.int32) - 1, jnp.sum(sums, axis=0, keepdims=True).astype(jnp.int32)

    rim_most = jnp.zeros((1, 1), jnp.int32)
    all_list, low_list = [], []
    for j in range(planes):
        ids, named, rim = flags(j)
        valid = refs[j][:block_count]
        counts = jnp.sum(valid, axis=1, keepdims=True)
        total = lambda m: jnp.sum(jnp.where(m, counts, 0), axis=0, keepdims=True)
        rim_most = jnp.maximum(rim_most, total(rim))
        all_list.append(total(named))
        low_list.append(total(named & (row_of < HB)))
        if j == 0:
            own_ids = ids
            rim_mask = jnp.where(rim, valid, 0)
            rest_mask = jnp.where(named & jnp.logical_not(rim), valid, 0)
            rim_rank, rim_count = ranks(rim_mask)
            rest_rank, _ = ranks(rest_mask)
            place = jnp.where(rim_mask > 0, rim_rank, jnp.where(rest_mask > 0, rest_rank + rim_count, -1))
        if j == 1:
            next_ids = ids
            next_mask = jnp.where(rim, valid, 0)
            next_rank, _ = ranks(next_mask)
            next_place = jnp.where(next_mask > 0, next_rank + NEXT, -1)
    branch = jnp.zeros((1, 1), jnp.int32) + (len(SIZES) - 1)
    for n in reversed(range(len(SIZES) - 1)):
        r, l = SIZES[n]
        fits = rim_most <= r
        for everything, low in zip(all_list, low_list):
            fits = fits & (everything - jnp.minimum(low, r) <= l)
        branch = jnp.where(fits, n, branch)
    size = jnp.zeros((1, 1), jnp.int32)
    for n, (r, _) in enumerate(SIZES):
        size = jnp.where(branch == n, r, size)
    behind = jnp.where(row_of >= HB, jnp.maximum(size - low_list[0], 0), 0)
    place = jnp.where(place >= 0, place + behind + whole_tiles(size) - size, -1)
    place_ref[...] = place

    def look(block):
        here = jnp.max(jnp.where(own_ids == block, place, -1), axis=0, keepdims=True)
        beyond = jnp.max(jnp.where(next_ids == block, next_place, -1), axis=0, keepdims=True)
        return jnp.maximum(here, beyond)

    found = [look(firsts[0][:, p : p + 1]) for p in range(pairs)] + [look(partners[0][:, p : p + 1]) for p in range(pairs)]
    found = jnp.concatenate(found, 0)
    where_ref[...] = found
    starts = jnp.min(jnp.where(found >= 0, found, 2 * NEXT), axis=1, keepdims=True)
    starts = jnp.where(starts == 2 * NEXT, 0, starts)
    lanes = lax.broadcasted_iota(jnp.int32, info_ref.shape, 1)
    info_ref[...] = jnp.where(lanes == 0, starts, branch)


def plan(me, own, others, block_count, pairs):
    vmem = pl.BlockSpec(memory_space=pltpu.VMEM)
    return pl.pallas_call(
        lambda *refs: plan_kernel(block_count, *refs),
        in_specs=[pl.BlockSpec(memory_space=pltpu.SMEM)] + [vmem] * 4,
        out_specs=[vmem] * 3,
        out_shape=[
            jax.ShapeDtypeStruct((block_count, WIDTH), jnp.int32),
            jax.ShapeDtypeStruct((2 * pairs, WIDTH), jnp.int32),
            jax.ShapeDtypeStruct((2 * pairs, WIDTH), jnp.int32),
        ],
    )(me, own, *others)


def spectra_kernel(base, count, tile, across, place_ref, samples_ref, table_ref, out_ref, held, table, picked, spectra, power, held_sem, table_sem):
    segs, channels, samples_len = held.shape
    lanes = picked.shape[0]
    pieces = table_sem.shape[0]
    rows = table.shape[0] // pieces

    get = [pltpu.make_async_copy(samples_ref.at[s, :channels, :], held.at[s], held_sem.at[s]) for s in range(segs)]
    for copy in get:
        copy.start()

    def table_copy(n):
        here = pl.ds(pl.multiple_of(n * rows, rows), rows)
        return pltpu.make_async_copy(table_ref.at[here, :], table.at[here, :], table_sem.at[n])

    @pl.loop(0, pieces)
    def _(n):
        table_copy(n).start()

    target = lax.broadcasted_iota(jnp.int32, (count, channels), 0) + base
    chosen = (place_ref[:, :channels] == target).astype(jnp.bfloat16)
    for s in range(segs):
        get[s].wait()

        @pl.loop(0, samples_len // tile)
        def _(n):
            cols = pl.ds(pl.multiple_of(n * tile, tile), tile)
            found = jnp.dot(chosen, held[s, :, cols], preferred_element_type=jnp.float32)
            picked[s * count : (s + 1) * count, cols] = found.astype(jnp.bfloat16)

    power[...] = jnp.zeros(power.shape, jnp.float32)

    @pl.loop(0, pieces)
    def _(n):
        here = pl.ds(pl.multiple_of(n * rows, rows), rows)
        table_copy(n).wait()

        @pl.loop(0, lanes // across)
        def _(m):
            cols = pl.ds(pl.multiple_of(m * across, across), across)
            block = lax.dot_general(
                table[here, :], picked[cols, :], (((1,), (1,)), ((), ())), preferred_element_type=jnp.float32
            )
            spectra[here, cols] = block
            power[:, cols] = power[:, cols] + jnp.sum((block * block).reshape(rows // 8, 8, across), axis=0)

    scale = lax.rsqrt(jnp.sum(power[...], axis=0, keepdims=True) / (table.shape[0] // 2) + 1e-06)
    peers, each, _ = out_ref.shape

    @pl.loop(0, peers)
    def _(peer):
        here = pl.ds(pl.multiple_of(peer * each, each), each)
        out_ref[peer] = (spectra[here, : segs * count] * scale[:, : segs * count]).astype(jnp.bfloat16)


def spectra_chunk(samples, table, place, channels, base, count, peers, urgent):
    segs, _, samples_len = samples.shape
    rows_total = table.shape[0]
    lanes = segs * count
    pieces, tile, across = (4, 1024, lanes) if urgent else (4, 256, 256)
    wide = (lanes + across - 1) // across * across
    body = lambda *refs: spectra_kernel(base, count, tile, across, *refs)
    hbm = pl.BlockSpec(memory_space=pl.ANY)
    vmem = pl.BlockSpec(memory_space=pltpu.VMEM)
    return pl.pallas_call(
        body,
        in_specs=[vmem, hbm, hbm],
        out_specs=vmem,
        out_shape=jax.ShapeDtypeStruct((peers, rows_total // peers, lanes), jnp.bfloat16),
        scratch_shapes=[
            pltpu.VMEM((segs, channels, samples_len), jnp.bfloat16),
            pltpu.VMEM((rows_total, samples_len), jnp.bfloat16),
            pltpu.VMEM((wide, samples_len), jnp.bfloat16),
            pltpu.VMEM((rows_total, wide), jnp.float32),
            pltpu.VMEM((8, wide), jnp.float32),
            pltpu.SemaphoreType.DMA((segs,)),
            pltpu.SemaphoreType.DMA((pieces,)),
        ],
        compiler_params=pltpu.CompilerParams(vmem_limit_bytes=VMEM + 7 * 512 * 1024),
        cost_estimate=pl.CostEstimate(
            flops=2 * segs * count * samples_len * (rows_total + channels),
            bytes_accessed=2 * (segs * channels * samples_len + rows_total * samples_len),
            transcendentals=0,
        ),
    )(place, samples, table)


def after(value, other):
    def nothing(value_ref, other_ref, out_ref):
        del value_ref, other_ref, out_ref

    anywhere = pl.BlockSpec(memory_space=pl.ANY)
    return pl.pallas_call(
        nothing,
        in_specs=[anywhere, anywhere],
        out_specs=anywhere,
        out_shape=jax.ShapeDtypeStruct(value.shape, value.dtype),
        input_output_aliases={0: 0},
        compiler_params=pltpu.CompilerParams(vmem_limit_bytes=VMEM + 7 * 512 * 1024),
        cost_estimate=pl.CostEstimate(flops=10**11, bytes_accessed=2**30, transcendentals=0),
    )(value, other)


def stack_kernel(counts, scale, info_ref, where_ref, regroup_ref, xr_ref, xl_ref, zr_ref, out_ref, pick_l, pick_r, held):
    r_count, l_count = counts
    own = whole_tiles(r_count) + whole_tiles(l_count)
    pairs, bins, _, width, _ = out_ref.shape
    window = 2 * width
    behind = own + whole_tiles(r_count) - r_count - NEXT

    def start(n):
        first = info_ref[n, 0]
        first = jnp.where(first >= NEXT, first + behind, first)
        return pl.multiple_of((first // width) * width, width)

    @pl.when(pl.program_id(0) == 0)
    def _():
        held[:, held.shape[1] - width :] = jnp.zeros((held.shape[0], width), held.dtype)
        where = where_ref[...]
        where = jnp.where(where >= NEXT, where + behind, where)
        eye = lax.broadcasted_iota(jnp.int32, (width, width), 0) == lax.broadcasted_iota(jnp.int32, (width, width), 1)
        for p in range(pairs):
            pick_l[p] = (where[p : p + 1] == lax.broadcasted_iota(jnp.int32, (window, width), 0) + start(p)).astype(jnp.bfloat16) * jnp.bfloat16(scale)
            row = where[pairs + p : pairs + p + 1]
            pick_r[p] = (row == lax.broadcasted_iota(jnp.int32, (window, width), 0) + start(pairs + p)).astype(jnp.bfloat16)

    chunks = ((xr_ref, r_count, 0, True), (xl_ref, l_count, whole_tiles(r_count), False), (zr_ref, r_count, own, True))
    for ref, count, at, to_end in chunks:
        full = whole_tiles(count)
        for h in range(2):
            rows = ref[h * 16 : (h + 1) * 16].reshape(256, 2 * count)
            rows = jnp.dot(regroup_ref[...], rows, preferred_element_type=jnp.float32)
            by_seg = [rows[:, :full], rows[:, 2 * count - full :]]
            if full != count:
                turn = 0 if to_end else 1
                by_seg[turn] = pltpu.roll(by_seg[turn], WIDTH // 2 if to_end else full - WIDTH // 2, 1)
            for s in range(2):
                part = by_seg[s].astype(jnp.bfloat16)
                for k in range(bins):
                    to = k * 128 + (s * 2 + h) * 32
                    held[to : to + 32, at : at + full] = part[k * 32 : (k + 1) * 32]

    def one_pair(p):
        from_l = held[:, pl.ds(start(p), window)]
        left = jnp.dot(from_l, pick_l[p], preferred_element_type=jnp.float32)
        left = left.astype(jnp.bfloat16)
        from_r = held[:, pl.ds(start(pairs + p), window)]
        right = jnp.dot(from_r, pick_r[p], preferred_element_type=jnp.float32).astype(jnp.bfloat16)
        for k in range(bins):
            b = right[k * 128 : (k + 1) * 128]
            turned = []
            for g in range(4):
                turned.append(-b[g * 32 + 16 : g * 32 + 32])
                turned.append(b[g * 32 : g * 32 + 16])
            both = jnp.concatenate([b, jnp.concatenate(turned, 0)], 1)
            a = left[k * 128 : (k + 1) * 128]
            res = (lax.dot_general(a, both, (((0,), (0,)), ((), ())), preferred_element_type=jnp.float32)).astype(jnp.bfloat16)
            out_ref[p, k, 0] = res[:, :width]
            out_ref[p, k, 1] = res[:, width:]

    pl.loop(0, pairs, unroll=4 if r_count < 256 else 2 if r_count < 320 else 1)(one_pair)


def stacked_products(xr, xl, zr, info, where, regroup, pairs, scale):
    peers, rows, r_two = xr.shape
    l_two = xl.shape[2]
    r_count, l_count = r_two // 2, l_two // 2
    bins = rows // 2
    group = 8
    body = lambda *refs: stack_kernel((r_count, l_count), scale, *refs)
    whole = lambda shape: pl.BlockSpec(shape, lambda g: (0,) * len(shape))
    part = lambda lanes: pl.BlockSpec((peers, 2 * group, lanes), lambda g: (0, g, 0))
    return pl.pallas_call(
        body,
        grid=(bins // group,),
        in_specs=[
            pl.BlockSpec(memory_space=pltpu.SMEM), whole(where.shape), whole((256, 256)),
            part(r_two), part(l_two), part(r_two),
        ],
        out_specs=pl.BlockSpec((pairs, group, 2, WIDTH, WIDTH), lambda g: (0, g, 0, 0, 0)),
        out_shape=jax.ShapeDtypeStruct((pairs, bins, 2, WIDTH, WIDTH), jnp.bfloat16),
        scratch_shapes=[
            pltpu.VMEM((pairs, 2 * WIDTH, WIDTH), jnp.bfloat16),
            pltpu.VMEM((pairs, 2 * WIDTH, WIDTH), jnp.bfloat16),
            pltpu.VMEM((group * 128, 2 * whole_tiles(r_count) + whole_tiles(l_count) + WIDTH), jnp.bfloat16),
        ],
        compiler_params=pltpu.CompilerParams(vmem_limit_bytes=VMEM),
        cost_estimate=pl.CostEstimate(
            flops=2 * peers * rows * 2 * WIDTH * (4 * pairs * WIDTH + 2 * r_two + l_two),
            bytes_accessed=2 * (peers * rows * (2 * r_two + l_two) + pairs * bins * 2 * WIDTH * WIDTH),
            transcendentals=0,
        ),
    )(info, where, regroup, xr, xl, zr)


def shards(samples, valid_counts, channel_mask, block_pairs):
    segs, channels, samples_len = samples.shape
    block_count = valid_counts.shape[0]
    planes = lax.axis_size("blk")
    peers = lax.axis_size("seg") * lax.axis_size("freq")
    pairs = block_pairs.shape[0]
    bins = samples_len // 2

    table, regroup = lax.optimization_barrier(
        (jnp.asarray(transform_table(bins, samples_len)), jnp.asarray(regroup_matrix()))
    )
    within = jnp.arange(WIDTH, dtype=jnp.int32)[None, :] < valid_counts[:, None]
    valid = (within & (channel_mask.reshape(block_count, WIDTH) == 1)).astype(jnp.int32)
    lines = jnp.pad(block_pairs.T, ((0, block_count - 2), (0, WIDTH - pairs)))
    own = jnp.concatenate([valid, lines], 0)
    others = [
        lax.ppermute(own, "blk", [(i, (i - shift) % planes) for i in range(planes)]) for shift in range(1, planes)
    ]
    me = lax.axis_index("blk").astype(jnp.int32).reshape(1, 1)
    place, where, info = plan(me, own, others, block_count, pairs)
    place_row = place.reshape(1, channels)
    scale = 1.0 / math.sqrt(peers * segs)

    def with_sizes(r_count, l_count):
        def run(samples, table, regroup, place_row, where, info):
            own_r = spectra_chunk(samples, table, place_row, HB * WIDTH, whole_tiles(r_count) - r_count, r_count, peers, r_count < 320)
            xr = lax.all_to_all(own_r, ("seg", "freq"), split_axis=0, concat_axis=0, tiled=True)
            own_l = spectra_chunk(samples, table, place_row, channels, whole_tiles(r_count), l_count, peers, False)
            xr, own_l = lax.optimization_barrier((xr, own_l))
            zr = lax.ppermute(xr, "blk", [(i, i - 1) for i in range(1, planes)])
            zr = after(zr, info)
            xl = lax.all_to_all(own_l, ("seg", "freq"), split_axis=0, concat_axis=0, tiled=True)
            return stacked_products(xr, xl, zr, info, where, regroup, pairs, scale)

        return run

    return lax.switch(
        info[0, 1],
        [with_sizes(r, l) for r, l in SIZES],
        samples, table, regroup, place_row, where, info,
    )


def solution(mesh):
    placed = (P(("seg", "freq"), "blk", None), P("blk"), P("blk"), P("blk", None))
    return jax.shard_map(
        shards,
        mesh=mesh,
        in_specs=placed,
        out_specs=P("blk", ("seg", "freq"), None, None, None),
        check_vma=False,
    )
```

```python
import math

import jax
import jax.numpy as jnp
import numpy as np
from jax import lax
from jax.experimental import pallas as pl
from jax.experimental.pallas import tpu as pltpu
from jax.sharding import PartitionSpec as P

WIDTH = 128
HB = 4
SIZES = ((128, 320), (192, 320), (256, 448), (320, 448), (512, 512))
VMEM = 60 * 1024 * 1024
NEXT = 1 << 16


def transform_table(bins, samples_len):
    times = np.arange(samples_len, dtype=np.int64)
    order = np.arange(bins, dtype=np.int64)
    phase = (order[:, None] * times[None, :]) % samples_len
    angle = phase * (2.0 * math.pi / samples_len)
    taper = 0.5 - 0.5 * np.cos(times * (2.0 * math.pi / samples_len))
    table = np.stack([taper * np.cos(angle), -taper * np.sin(angle)], 1)
    return table.reshape(2 * bins, samples_len).astype(np.float32).astype(jnp.bfloat16)


def regroup_matrix():
    out = np.zeros((256, 256), np.float32)
    for src in range(16):
        for row in range(16):
            out[row * 16 + src, src * 16 + row] = 1.0
    return out.astype(jnp.bfloat16)


def whole_tiles(count):
    return (count + WIDTH - 1) // WIDTH * WIDTH


def plan_kernel(block_count, me_ref, own_ref, n1_ref, n2_ref, n3_ref, place_ref, where_ref, info_ref, branch_ref):
    refs = (own_ref, n1_ref, n2_ref, n3_ref)
    planes = len(refs)
    me = me_ref[0, 0]
    pairs = where_ref.shape[0] // 2
    firsts = [ref[block_count : block_count + 1, :pairs] for ref in refs]
    partners = [ref[block_count + 1 : block_count + 2, :pairs] for ref in refs]
    flat = lambda x: x.astype(jnp.float32).astype(jnp.bfloat16)
    upto = flat(
        (lax.broadcasted_iota(jnp.int32, (WIDTH, WIDTH), 0) <= lax.broadcasted_iota(jnp.int32, (WIDTH, WIDTH), 1)).astype(jnp.int32)
    )
    row_of = lax.broadcasted_iota(jnp.int32, (block_count, 1), 0)

    def flags(j):
        ids = row_of + lax.rem(me + j, planes) * block_count
        named = jnp.zeros((block_count, 1), jnp.int32)
        rim = jnp.zeros((block_count, 1), jnp.int32)
        for first, partner in zip(firsts, partners):
            hit = partner == ids
            crosses = (first // block_count) != (partner // block_count)
            named = named + jnp.sum((hit | (first == ids)).astype(jnp.int32), axis=1, keepdims=True)
            rim = rim + jnp.sum((hit & crosses).astype(jnp.int32), axis=1, keepdims=True)
        return ids, named > 0, rim > 0

    def ranks(chosen):
        inside = jnp.dot(flat(chosen), upto, preferred_element_type=jnp.float32)
        sums = inside[:, WIDTH - 1 :]
        before = jnp.zeros((block_count, 1), jnp.float32)
        for b in range(block_count - 1):
            before = before + jnp.where(row_of > b, sums[b : b + 1], 0.0)
        return (inside + before).astype(jnp.int32) - 1, jnp.sum(sums, axis=0, keepdims=True).astype(jnp.int32)

    rim_most = jnp.zeros((1, 1), jnp.int32)
    all_list, low_list = [], []
    for j in range(planes):
        ids, named, rim = flags(j)
        valid = refs[j][:block_count]
        counts = jnp.sum(valid, axis=1, keepdims=True)
        total = lambda m: jnp.sum(jnp.where(m, counts, 0), axis=0, keepdims=True)
        rim_most = jnp.maximum(rim_most, total(rim))
        all_list.append(total(named))
        low_list.append(total(named & (row_of < HB)))
        if j == 0:
            own_ids = ids
            rim_mask = jnp.where(rim, valid, 0)
            rest_mask = jnp.where(named & jnp.logical_not(rim), valid, 0)
            rim_rank, rim_count = ranks(rim_mask)
            rest_rank, _ = ranks(rest_mask)
            place = jnp.where(rim_mask > 0, rim_rank, jnp.where(rest_mask > 0, rest_rank + rim_count, -1))
        if j == 1:
            next_ids = ids
            next_mask = jnp.where(rim, valid, 0)
            next_rank, _ = ranks(next_mask)
            next_place = jnp.where(next_mask > 0, next_rank + NEXT, -1)
    branch = jnp.zeros((1, 1), jnp.int32) + (len(SIZES) - 1)
    for n in reversed(range(len(SIZES) - 1)):
        r, l = SIZES[n]
        fits = rim_most <= r
        for everything, low in zip(all_list, low_list):
            fits = fits & (everything - jnp.minimum(low, r) <= l)
        branch = jnp.where(fits, n, branch)
    size = jnp.zeros((1, 1), jnp.int32)
    for n, (r, _) in enumerate(SIZES):
        size = jnp.where(branch == n, r, size)
    behind = jnp.where(row_of >= HB, jnp.maximum(size - low_list[0], 0), 0)
    place = jnp.where(place >= 0, place + behind + whole_tiles(size) - size, -1)
    place_ref[...] = place

    def look(block):
        here = jnp.max(jnp.where(own_ids == block, place, -1), axis=0, keepdims=True)
        beyond = jnp.max(jnp.where(next_ids == block, next_place, -1), axis=0, keepdims=True)
        return jnp.maximum(here, beyond)

    found = [look(firsts[0][:, p : p + 1]) for p in range(pairs)] + [look(partners[0][:, p : p + 1]) for p in range(pairs)]
    found = jnp.concatenate(found, 0)
    where_ref[...] = found
    starts = jnp.min(jnp.where(found >= 0, found, 2 * NEXT), axis=1, keepdims=True)
    starts = jnp.where(starts == 2 * NEXT, 0, starts)
    lanes = lax.broadcasted_iota(jnp.int32, info_ref.shape, 1)
    info_ref[...] = jnp.where(lanes == 0, starts, 0)
    branch_ref[0, 0] = jnp.max(branch)


def plan(me, own, others, block_count, pairs):
    vmem = pl.BlockSpec(memory_space=pltpu.VMEM)
    return pl.pallas_call(
        lambda *refs: plan_kernel(block_count, *refs),
        in_specs=[pl.BlockSpec(memory_space=pltpu.SMEM)] + [vmem] * 4,
        out_specs=[vmem] * 3 + [pl.BlockSpec(memory_space=pltpu.SMEM)],
        out_shape=[
            jax.ShapeDtypeStruct((block_count, WIDTH), jnp.int32),
            jax.ShapeDtypeStruct((2 * pairs, WIDTH), jnp.int32),
            jax.ShapeDtypeStruct((2 * pairs, WIDTH), jnp.int32),
            jax.ShapeDtypeStruct((1, 1), jnp.int32),
        ],
    )(me, own, *others)


def spectra_kernel(base, count, tile, across, place_ref, samples_ref, table_ref, out_ref, held, table, picked, spectra, power, ready, held_sem, table_sem, out_sem):
    segs, channels, samples_len = held.shape
    lanes = picked.shape[0]
    pieces = table_sem.shape[0]
    rows = table.shape[0] // pieces

    get = [pltpu.make_async_copy(samples_ref.at[s, :channels, :], held.at[s], held_sem.at[s]) for s in range(segs)]
    for copy in get:
        copy.start()

    def table_copy(n):
        here = pl.ds(pl.multiple_of(n * rows, rows), rows)
        return pltpu.make_async_copy(table_ref.at[here, :], table.at[here, :], table_sem.at[n])

    @pl.loop(0, pieces)
    def _(n):
        table_copy(n).start()

    target = lax.broadcasted_iota(jnp.int32, (count, channels), 0) + base
    chosen = (place_ref[:, :channels] == target).astype(jnp.bfloat16)
    for s in range(segs):
        get[s].wait()

        @pl.loop(0, samples_len // tile)
        def _(n):
            cols = pl.ds(pl.multiple_of(n * tile, tile), tile)
            found = jnp.dot(chosen, held[s, :, cols], preferred_element_type=jnp.float32)
            picked[s * count : (s + 1) * count, cols] = found.astype(jnp.bfloat16)

    power[...] = jnp.zeros(power.shape, jnp.float32)

    @pl.loop(0, pieces)
    def _(n):
        here = pl.ds(pl.multiple_of(n * rows, rows), rows)
        table_copy(n).wait()

        @pl.loop(0, lanes // across)
        def _(m):
            cols = pl.ds(pl.multiple_of(m * across, across), across)
            block = lax.dot_general(
                table[here, :], picked[cols, :], (((1,), (1,)), ((), ())), preferred_element_type=jnp.float32
            )
            spectra[here, cols] = block
            power[:, cols] = power[:, cols] + jnp.sum((block * block).reshape(rows // 8, 8, across), axis=0)

    scale = lax.rsqrt(jnp.sum(power[...], axis=0, keepdims=True) / (table.shape[0] // 2) + 1e-06)
    peers, each, _ = ready.shape
    quarter = peers // out_sem.shape[0]

    def send(n):
        here = pl.ds(pl.multiple_of(n * quarter, quarter), quarter)
        return pltpu.make_async_copy(ready.at[here], out_ref.at[here], out_sem.at[n])

    @pl.loop(0, out_sem.shape[0])
    def _(n):
        @pl.loop(0, quarter)
        def _(j):
            peer = n * quarter + j
            here = pl.ds(pl.multiple_of(peer * each, each), each)
            ready[peer] = (spectra[here, : segs * count] * scale[:, : segs * count]).astype(jnp.bfloat16)

        send(n).start()

    @pl.loop(0, out_sem.shape[0])
    def _(n):
        send(n).wait()


def spectra_chunk(samples, table, place, channels, base, count, peers, urgent):
    segs, _, samples_len = samples.shape
    rows_total = table.shape[0]
    lanes = segs * count
    pieces, tile, across = (4, 1024, lanes) if urgent else (4, 256, 256)
    wide = (lanes + across - 1) // across * across
    body = lambda *refs: spectra_kernel(base, count, tile, across, *refs)
    hbm = pl.BlockSpec(memory_space=pl.ANY)
    vmem = pl.BlockSpec(memory_space=pltpu.VMEM)
    return pl.pallas_call(
        body,
        in_specs=[vmem, hbm, hbm],
        out_specs=hbm,
        out_shape=jax.ShapeDtypeStruct((peers, rows_total // peers, lanes), jnp.bfloat16),
        scratch_shapes=[
            pltpu.VMEM((segs, channels, samples_len), jnp.bfloat16),
            pltpu.VMEM((rows_total, samples_len), jnp.bfloat16),
            pltpu.VMEM((wide, samples_len), jnp.bfloat16),
            pltpu.VMEM((rows_total, wide), jnp.float32),
            pltpu.VMEM((8, wide), jnp.float32),
            pltpu.VMEM((peers, rows_total // peers, lanes), jnp.bfloat16),
            pltpu.SemaphoreType.DMA((segs,)),
            pltpu.SemaphoreType.DMA((pieces,)),
            pltpu.SemaphoreType.DMA((4,)),
        ],
        compiler_params=pltpu.CompilerParams(vmem_limit_bytes=VMEM + 7 * 512 * 1024),
        cost_estimate=pl.CostEstimate(
            flops=2 * segs * count * samples_len * (rows_total + channels),
            bytes_accessed=2 * (segs * channels * samples_len + rows_total * samples_len),
            transcendentals=0,
        ),
    )(place, samples, table)


def after(value, other):
    def nothing(value_ref, other_ref, out_ref):
        del value_ref, other_ref, out_ref

    anywhere = pl.BlockSpec(memory_space=pl.ANY)
    return pl.pallas_call(
        nothing,
        in_specs=[anywhere, anywhere],
        out_specs=anywhere,
        out_shape=jax.ShapeDtypeStruct(value.shape, value.dtype),
        input_output_aliases={0: 0},
        compiler_params=pltpu.CompilerParams(vmem_limit_bytes=VMEM + 7 * 512 * 1024),
        cost_estimate=pl.CostEstimate(flops=10**11, bytes_accessed=2**30, transcendentals=0),
    )(value, other)


def stack_kernel(counts, scale, info_ref, where_ref, regroup_ref, xr_ref, xl_ref, zr_ref, out_ref, pick_l, pick_r, held):
    r_count, l_count = counts
    own = whole_tiles(r_count) + whole_tiles(l_count)
    pairs, bins, _, width, _ = out_ref.shape
    window = 2 * width
    behind = own + whole_tiles(r_count) - r_count - NEXT

    def start(n):
        first = info_ref[n, 0]
        first = jnp.where(first >= NEXT, first + behind, first)
        return pl.multiple_of((first // width) * width, width)

    @pl.when(pl.program_id(0) == 0)
    def _():
        held[:, held.shape[1] - width :] = jnp.zeros((held.shape[0], width), held.dtype)
        where = where_ref[...]
        where = jnp.where(where >= NEXT, where + behind, where)
        eye = lax.broadcasted_iota(jnp.int32, (width, width), 0) == lax.broadcasted_iota(jnp.int32, (width, width), 1)
        for p in range(pairs):
            pick_l[p] = (where[p : p + 1] == lax.broadcasted_iota(jnp.int32, (window, width), 0) + start(p)).astype(jnp.bfloat16) * jnp.bfloat16(scale)
            row = where[pairs + p : pairs + p + 1]
            pick_r[p] = (row == lax.broadcasted_iota(jnp.int32, (window, width), 0) + start(pairs + p)).astype(jnp.bfloat16)

    chunks = ((xr_ref, r_count, 0, True), (xl_ref, l_count, whole_tiles(r_count), False), (zr_ref, r_count, own, True))
    for ref, count, at, to_end in chunks:
        full = whole_tiles(count)
        for h in range(2):
            rows = ref[h * 16 : (h + 1) * 16].reshape(256, 2 * count)
            rows = jnp.dot(regroup_ref[...], rows, preferred_element_type=jnp.float32)
            by_seg = [rows[:, :full], rows[:, 2 * count - full :]]
            if full != count:
                turn = 0 if to_end else 1
                by_seg[turn] = pltpu.roll(by_seg[turn], WIDTH // 2 if to_end else full - WIDTH // 2, 1)
            for s in range(2):
                part = by_seg[s].astype(jnp.bfloat16)
                for k in range(bins):
                    to = k * 128 + (s * 2 + h) * 32
                    held[to : to + 32, at : at + full] = part[k * 32 : (k + 1) * 32]

    def one_pair(p):
        from_l = held[:, pl.ds(start(p), window)]
        left = jnp.dot(from_l, pick_l[p], preferred_element_type=jnp.float32)
        left = left.astype(jnp.bfloat16)
        from_r = held[:, pl.ds(start(pairs + p), window)]
        right = jnp.dot(from_r, pick_r[p], preferred_element_type=jnp.float32).astype(jnp.bfloat16)
        for k in range(bins):
            b = right[k * 128 : (k + 1) * 128]
            turned = []
            for g in range(4):
                turned.append(-b[g * 32 + 16 : g * 32 + 32])
                turned.append(b[g * 32 : g * 32 + 16])
            both = jnp.concatenate([b, jnp.concatenate(turned, 0)], 1)
            a = left[k * 128 : (k + 1) * 128]
            res = (lax.dot_general(a, both, (((0,), (0,)), ((), ())), preferred_element_type=jnp.float32)).astype(jnp.bfloat16)
            out_ref[p, k, 0] = res[:, :width]
            out_ref[p, k, 1] = res[:, width:]

    pl.loop(0, pairs, unroll=4 if r_count < 256 else 1)(one_pair)


def stacked_products(xr, xl, zr, info, where, regroup, pairs, scale):
    peers, rows, r_two = xr.shape
    l_two = xl.shape[2]
    r_count, l_count = r_two // 2, l_two // 2
    bins = rows // 2
    group = 8
    body = lambda *refs: stack_kernel((r_count, l_count), scale, *refs)
    whole = lambda shape: pl.BlockSpec(shape, lambda g: (0,) * len(shape))
    part = lambda lanes: pl.BlockSpec((peers, 2 * group, lanes), lambda g: (0, g, 0))
    return pl.pallas_call(
        body,
        grid=(bins // group,),
        in_specs=[
            pl.BlockSpec(memory_space=pltpu.SMEM), whole(where.shape), whole((256, 256)),
            part(r_two), part(l_two), part(r_two),
        ],
        out_specs=pl.BlockSpec((pairs, group, 2, WIDTH, WIDTH), lambda g: (0, g, 0, 0, 0)),
        out_shape=jax.ShapeDtypeStruct((pairs, bins, 2, WIDTH, WIDTH), jnp.bfloat16),
        scratch_shapes=[
            pltpu.VMEM((pairs, 2 * WIDTH, WIDTH), jnp.bfloat16),
            pltpu.VMEM((pairs, 2 * WIDTH, WIDTH), jnp.bfloat16),
            pltpu.VMEM((group * 128, 2 * whole_tiles(r_count) + whole_tiles(l_count) + WIDTH), jnp.bfloat16),
        ],
        compiler_params=pltpu.CompilerParams(vmem_limit_bytes=VMEM),
        cost_estimate=pl.CostEstimate(
            flops=2 * peers * rows * 2 * WIDTH * (4 * pairs * WIDTH + 2 * r_two + l_two),
            bytes_accessed=2 * (peers * rows * (2 * r_two + l_two) + pairs * bins * 2 * WIDTH * WIDTH),
            transcendentals=0,
        ),
    )(info, where, regroup, xr, xl, zr)


def shards(samples, valid_counts, channel_mask, block_pairs):
    segs, channels, samples_len = samples.shape
    block_count = valid_counts.shape[0]
    planes = lax.axis_size("blk")
    peers = lax.axis_size("seg") * lax.axis_size("freq")
    pairs = block_pairs.shape[0]
    bins = samples_len // 2

    table, regroup = lax.optimization_barrier(
        (jnp.asarray(transform_table(bins, samples_len)), jnp.asarray(regroup_matrix()))
    )
    within = jnp.arange(WIDTH, dtype=jnp.int32)[None, :] < valid_counts[:, None]
    valid = (within & (channel_mask.reshape(block_count, WIDTH) == 1)).astype(jnp.int32)
    lines = jnp.pad(block_pairs.T, ((0, block_count - 2), (0, WIDTH - pairs)))
    own = jnp.concatenate([valid, lines], 0)
    others = [
        lax.ppermute(own, "blk", [(i, (i - shift) % planes) for i in range(planes)]) for shift in range(1, planes)
    ]
    me = lax.axis_index("blk").astype(jnp.int32).reshape(1, 1)
    place, where, info, branch = plan(me, own, others, block_count, pairs)
    place_row = place.reshape(1, channels)
    scale = 1.0 / math.sqrt(peers * segs)

    def with_sizes(r_count, l_count):
        def run(samples, table, regroup, place_row, where, info):
            own_r = spectra_chunk(samples, table, place_row, HB * WIDTH, whole_tiles(r_count) - r_count, r_count, peers, r_count < 320)
            xr = lax.all_to_all(own_r, ("seg", "freq"), split_axis=0, concat_axis=0, tiled=True)
            own_l = spectra_chunk(samples, table, place_row, channels, whole_tiles(r_count), l_count, peers, False)
            xr, own_l = lax.optimization_barrier((xr, own_l))
            zr = lax.ppermute(xr, "blk", [(i, i - 1) for i in range(1, planes)])
            info = after(info, zr)
            xl = lax.all_to_all(own_l, ("seg", "freq"), split_axis=0, concat_axis=0, tiled=True)
            return stacked_products(xr, xl, zr, info, where, regroup, pairs, scale)

        return run

    return lax.switch(
        branch[0, 0],
        [with_sizes(r, l) for r, l in SIZES],
        samples, table, regroup, place_row, where, info,
    )


def solution(mesh):
    placed = (P(("seg", "freq"), "blk", None), P("blk"), P("blk"), P("blk", None))
    return jax.shard_map(
        shards,
        mesh=mesh,
        in_specs=placed,
        out_specs=P("blk", ("seg", "freq"), None, None, None),
        check_vma=False,
    )
```

```python
import math

import jax
import jax.numpy as jnp
import numpy as np
from jax import lax
from jax.experimental import pallas as pl
from jax.experimental.pallas import tpu as pltpu
from jax.sharding import PartitionSpec as P

WIDTH = 128
HB = 4
SIZES = ((128, 320), (192, 320), (256, 448), (320, 448), (512, 512))
VMEM = 60 * 1024 * 1024
NEXT = 1 << 16


def transform_table(bins, samples_len):
    times = np.arange(samples_len, dtype=np.int64)
    order = np.arange(bins, dtype=np.int64)
    phase = (order[:, None] * times[None, :]) % samples_len
    angle = phase * (2.0 * math.pi / samples_len)
    taper = 0.5 - 0.5 * np.cos(times * (2.0 * math.pi / samples_len))
    table = np.stack([taper * np.cos(angle), -taper * np.sin(angle)], 1)
    return table.reshape(2 * bins, samples_len).astype(np.float32).astype(jnp.bfloat16)


def regroup_matrix():
    out = np.zeros((256, 256), np.float32)
    for src in range(16):
        for row in range(16):
            out[row * 16 + src, src * 16 + row] = 1.0
    return out.astype(jnp.bfloat16)


def whole_tiles(count):
    return (count + WIDTH - 1) // WIDTH * WIDTH


def plan_kernel(block_count, me_ref, own_ref, n1_ref, n2_ref, n3_ref, place_ref, where_ref, info_ref, branch_ref):
    refs = (own_ref, n1_ref, n2_ref, n3_ref)
    planes = len(refs)
    me = me_ref[0, 0]
    pairs = where_ref.shape[0] // 2
    firsts = [ref[block_count : block_count + 1, :pairs] for ref in refs]
    partners = [ref[block_count + 1 : block_count + 2, :pairs] for ref in refs]
    flat = lambda x: x.astype(jnp.float32).astype(jnp.bfloat16)
    upto = flat(
        (lax.broadcasted_iota(jnp.int32, (WIDTH, WIDTH), 0) <= lax.broadcasted_iota(jnp.int32, (WIDTH, WIDTH), 1)).astype(jnp.int32)
    )
    row_of = lax.broadcasted_iota(jnp.int32, (block_count, 1), 0)

    def flags(j):
        ids = row_of + lax.rem(me + j, planes) * block_count
        named = jnp.zeros((block_count, 1), jnp.int32)
        rim = jnp.zeros((block_count, 1), jnp.int32)
        for first, partner in zip(firsts, partners):
            hit = partner == ids
            crosses = (first // block_count) != (partner // block_count)
            named = named + jnp.sum((hit | (first == ids)).astype(jnp.int32), axis=1, keepdims=True)
            rim = rim + jnp.sum((hit & crosses).astype(jnp.int32), axis=1, keepdims=True)
        return ids, named > 0, rim > 0

    def ranks(chosen):
        inside = jnp.dot(flat(chosen), upto, preferred_element_type=jnp.float32)
        sums = inside[:, WIDTH - 1 :]
        before = jnp.zeros((block_count, 1), jnp.float32)
        for b in range(block_count - 1):
            before = before + jnp.where(row_of > b, sums[b : b + 1], 0.0)
        return (inside + before).astype(jnp.int32) - 1, jnp.sum(sums, axis=0, keepdims=True).astype(jnp.int32)

    rim_most = jnp.zeros((1, 1), jnp.int32)
    all_list, low_list = [], []
    for j in range(planes):
        ids, named, rim = flags(j)
        valid = refs[j][:block_count]
        counts = jnp.sum(valid, axis=1, keepdims=True)
        total = lambda m: jnp.sum(jnp.where(m, counts, 0), axis=0, keepdims=True)
        rim_most = jnp.maximum(rim_most, total(rim))
        all_list.append(total(named))
        low_list.append(total(named & (row_of < HB)))
        if j == 0:
            own_ids = ids
            rim_mask = jnp.where(rim, valid, 0)
            rest_mask = jnp.where(named & jnp.logical_not(rim), valid, 0)
            rim_rank, rim_count = ranks(rim_mask)
            rest_rank, _ = ranks(rest_mask)
            place = jnp.where(rim_mask > 0, rim_rank, jnp.where(rest_mask > 0, rest_rank + rim_count, -1))
        if j == 1:
            next_ids = ids
            next_mask = jnp.where(rim, valid, 0)
            next_rank, _ = ranks(next_mask)
            next_place = jnp.where(next_mask > 0, next_rank + NEXT, -1)
    branch = jnp.zeros((1, 1), jnp.int32) + (len(SIZES) - 1)
    for n in reversed(range(len(SIZES) - 1)):
        r, l = SIZES[n]
        fits = rim_most <= r
        for everything, low in zip(all_list, low_list):
            fits = fits & (everything - jnp.minimum(low, r) <= l)
        branch = jnp.where(fits, n, branch)
    size = jnp.zeros((1, 1), jnp.int32)
    for n, (r, _) in enumerate(SIZES):
        size = jnp.where(branch == n, r, size)
    behind = jnp.where(row_of >= HB, jnp.maximum(size - low_list[0], 0), 0)
    place = jnp.where(place >= 0, place + behind + whole_tiles(size) - size, -1)
    place_ref[...] = place

    def look(block):
        here = jnp.max(jnp.where(own_ids == block, place, -1), axis=0, keepdims=True)
        beyond = jnp.max(jnp.where(next_ids == block, next_place, -1), axis=0, keepdims=True)
        return jnp.maximum(here, beyond)

    found = [look(firsts[0][:, p : p + 1]) for p in range(pairs)] + [look(partners[0][:, p : p + 1]) for p in range(pairs)]
    found = jnp.concatenate(found, 0)
    where_ref[...] = found
    starts = jnp.min(jnp.where(found >= 0, found, 2 * NEXT), axis=1, keepdims=True)
    starts = jnp.where(starts == 2 * NEXT, 0, starts)
    lanes = lax.broadcasted_iota(jnp.int32, info_ref.shape, 1)
    info_ref[...] = jnp.where(lanes == 0, starts, 0)
    branch_ref[0, 0] = jnp.max(branch)


def plan(me, own, others, block_count, pairs):
    vmem = pl.BlockSpec(memory_space=pltpu.VMEM)
    return pl.pallas_call(
        lambda *refs: plan_kernel(block_count, *refs),
        in_specs=[pl.BlockSpec(memory_space=pltpu.SMEM)] + [vmem] * 4,
        out_specs=[vmem] * 3 + [pl.BlockSpec(memory_space=pltpu.SMEM)],
        out_shape=[
            jax.ShapeDtypeStruct((block_count, WIDTH), jnp.int32),
            jax.ShapeDtypeStruct((2 * pairs, WIDTH), jnp.int32),
            jax.ShapeDtypeStruct((2 * pairs, WIDTH), jnp.int32),
            jax.ShapeDtypeStruct((1, 1), jnp.int32),
        ],
    )(me, own, *others)


def spectra_kernel(base, count, tile, across, place_ref, samples_ref, table_ref, out_ref, held, table, picked, spectra, power, ready, held_sem, table_sem, out_sem):
    segs, channels, samples_len = held.shape
    lanes = picked.shape[0]
    pieces = table_sem.shape[0]
    rows = table.shape[0] // pieces

    get = [pltpu.make_async_copy(samples_ref.at[s, :channels, :], held.at[s], held_sem.at[s]) for s in range(segs)]
    for copy in get:
        copy.start()

    def table_copy(n):
        here = pl.ds(pl.multiple_of(n * rows, rows), rows)
        return pltpu.make_async_copy(table_ref.at[here, :], table.at[here, :], table_sem.at[n])

    @pl.loop(0, pieces)
    def _(n):
        table_copy(n).start()

    target = lax.broadcasted_iota(jnp.int32, (count, channels), 0) + base
    chosen = (place_ref[:, :channels] == target).astype(jnp.bfloat16)
    for s in range(segs):
        get[s].wait()

        @pl.loop(0, samples_len // tile)
        def _(n):
            cols = pl.ds(pl.multiple_of(n * tile, tile), tile)
            found = jnp.dot(chosen, held[s, :, cols], preferred_element_type=jnp.float32)
            picked[s * count : (s + 1) * count, cols] = found.astype(jnp.bfloat16)

    power[...] = jnp.zeros(power.shape, jnp.float32)

    @pl.loop(0, pieces)
    def _(n):
        here = pl.ds(pl.multiple_of(n * rows, rows), rows)
        table_copy(n).wait()

        @pl.loop(0, lanes // across)
        def _(m):
            cols = pl.ds(pl.multiple_of(m * across, across), across)
            block = lax.dot_general(
                table[here, :], picked[cols, :], (((1,), (1,)), ((), ())), preferred_element_type=jnp.float32
            )
            spectra[here, cols] = block
            power[:, cols] = power[:, cols] + jnp.sum((block * block).reshape(rows // 8, 8, across), axis=0)

    scale = lax.rsqrt(jnp.sum(power[...], axis=0, keepdims=True) / (table.shape[0] // 2) + 1e-06)
    peers, each, _ = ready.shape
    quarter = peers // out_sem.shape[0]

    def send(n):
        here = pl.ds(pl.multiple_of(n * quarter, quarter), quarter)
        return pltpu.make_async_copy(ready.at[here], out_ref.at[here], out_sem.at[n])

    @pl.loop(0, out_sem.shape[0])
    def _(n):
        @pl.loop(0, quarter)
        def _(j):
            peer = n * quarter + j
            here = pl.ds(pl.multiple_of(peer * each, each), each)
            ready[peer] = (spectra[here, : segs * count] * scale[:, : segs * count]).astype(jnp.bfloat16)

        send(n).start()

    @pl.loop(0, out_sem.shape[0])
    def _(n):
        send(n).wait()


def spectra_chunk(samples, table, place, channels, base, count, peers, urgent):
    segs, _, samples_len = samples.shape
    rows_total = table.shape[0]
    lanes = segs * count
    pieces, tile, across = (4, 1024, lanes) if urgent else (4, 512 if count <= 320 and channels > HB * WIDTH else 256, 256)
    wide = (lanes + across - 1) // across * across
    body = lambda *refs: spectra_kernel(base, count, tile, across, *refs)
    hbm = pl.BlockSpec(memory_space=pl.ANY)
    vmem = pl.BlockSpec(memory_space=pltpu.VMEM)
    return pl.pallas_call(
        body,
        in_specs=[vmem, hbm, hbm],
        out_specs=hbm,
        out_shape=jax.ShapeDtypeStruct((peers, rows_total // peers, lanes), jnp.bfloat16),
        scratch_shapes=[
            pltpu.VMEM((segs, channels, samples_len), jnp.bfloat16),
            pltpu.VMEM((rows_total, samples_len), jnp.bfloat16),
            pltpu.VMEM((wide, samples_len), jnp.bfloat16),
            pltpu.VMEM((rows_total, wide), jnp.float32),
            pltpu.VMEM((8, wide), jnp.float32),
            pltpu.VMEM((peers, rows_total // peers, lanes), jnp.bfloat16),
            pltpu.SemaphoreType.DMA((segs,)),
            pltpu.SemaphoreType.DMA((pieces,)),
            pltpu.SemaphoreType.DMA((4,)),
        ],
        compiler_params=pltpu.CompilerParams(vmem_limit_bytes=VMEM + 7 * 512 * 1024),
        cost_estimate=pl.CostEstimate(
            flops=2 * segs * count * samples_len * (rows_total + channels),
            bytes_accessed=2 * (segs * channels * samples_len + rows_total * samples_len),
            transcendentals=0,
        ),
    )(place, samples, table)


def after(value, other):
    def nothing(value_ref, other_ref, out_ref):
        del value_ref, other_ref, out_ref

    anywhere = pl.BlockSpec(memory_space=pl.ANY)
    return pl.pallas_call(
        nothing,
        in_specs=[anywhere, anywhere],
        out_specs=anywhere,
        out_shape=jax.ShapeDtypeStruct(value.shape, value.dtype),
        input_output_aliases={0: 0},
        compiler_params=pltpu.CompilerParams(vmem_limit_bytes=VMEM + 7 * 512 * 1024),
        cost_estimate=pl.CostEstimate(flops=10**11, bytes_accessed=2**30, transcendentals=0),
    )(value, other)


def stack_kernel(counts, scale, info_ref, where_ref, regroup_ref, xr_ref, xl_ref, zr_ref, out_ref, pick_l, pick_r, held):
    r_count, l_count = counts
    own = whole_tiles(r_count) + whole_tiles(l_count)
    pairs, bins, _, width, _ = out_ref.shape
    window = 2 * width
    behind = own + whole_tiles(r_count) - r_count - NEXT

    def start(n):
        first = info_ref[n, 0]
        first = jnp.where(first >= NEXT, first + behind, first)
        return pl.multiple_of((first // width) * width, width)

    @pl.when(pl.program_id(0) == 0)
    def _():
        held[:, held.shape[1] - width :] = jnp.zeros((held.shape[0], width), held.dtype)
        where = where_ref[...]
        where = jnp.where(where >= NEXT, where + behind, where)
        eye = lax.broadcasted_iota(jnp.int32, (width, width), 0) == lax.broadcasted_iota(jnp.int32, (width, width), 1)
        for p in range(pairs):
            pick_l[p] = (where[p : p + 1] == lax.broadcasted_iota(jnp.int32, (window, width), 0) + start(p)).astype(jnp.bfloat16) * jnp.bfloat16(scale)
            row = where[pairs + p : pairs + p + 1]
            pick_r[p] = (row == lax.broadcasted_iota(jnp.int32, (window, width), 0) + start(pairs + p)).astype(jnp.bfloat16)

    chunks = ((xr_ref, r_count, 0, True), (xl_ref, l_count, whole_tiles(r_count), False), (zr_ref, r_count, own, True))
    for ref, count, at, to_end in chunks:
        full = whole_tiles(count)
        for h in range(2):
            rows = ref[h * 16 : (h + 1) * 16].reshape(256, 2 * count)
            rows = jnp.dot(regroup_ref[...], rows, preferred_element_type=jnp.float32)
            by_seg = [rows[:, :full], rows[:, 2 * count - full :]]
            if full != count:
                turn = 0 if to_end else 1
                by_seg[turn] = pltpu.roll(by_seg[turn], WIDTH // 2 if to_end else full - WIDTH // 2, 1)
            for s in range(2):
                part = by_seg[s].astype(jnp.bfloat16)
                for k in range(bins):
                    to = k * 128 + (s * 2 + h) * 32
                    held[to : to + 32, at : at + full] = part[k * 32 : (k + 1) * 32]

    def one_pair(p):
        from_l = held[:, pl.ds(start(p), window)]
        left = jnp.dot(from_l, pick_l[p], preferred_element_type=jnp.float32)
        left = left.astype(jnp.bfloat16)
        from_r = held[:, pl.ds(start(pairs + p), window)]
        right = jnp.dot(from_r, pick_r[p], preferred_element_type=jnp.float32).astype(jnp.bfloat16)
        for k in range(bins):
            b = right[k * 128 : (k + 1) * 128]
            turned = []
            for g in range(4):
                turned.append(-b[g * 32 + 16 : g * 32 + 32])
                turned.append(b[g * 32 : g * 32 + 16])
            both = jnp.concatenate([b, jnp.concatenate(turned, 0)], 1)
            a = left[k * 128 : (k + 1) * 128]
            res = (lax.dot_general(a, both, (((0,), (0,)), ((), ())), preferred_element_type=jnp.float32)).astype(jnp.bfloat16)
            out_ref[p, k, 0] = res[:, :width]
            out_ref[p, k, 1] = res[:, width:]

    pl.loop(0, pairs, unroll=4 if r_count < 256 else 1)(one_pair)


def stacked_products(xr, xl, zr, info, where, regroup, pairs, scale):
    peers, rows, r_two = xr.shape
    l_two = xl.shape[2]
    r_count, l_count = r_two // 2, l_two // 2
    bins = rows // 2
    group = 8
    body = lambda *refs: stack_kernel((r_count, l_count), scale, *refs)
    whole = lambda shape: pl.BlockSpec(shape, lambda g: (0,) * len(shape))
    part = lambda lanes: pl.BlockSpec((peers, 2 * group, lanes), lambda g: (0, g, 0))
    return pl.pallas_call(
        body,
        grid=(bins // group,),
        in_specs=[
            pl.BlockSpec(memory_space=pltpu.SMEM), whole(where.shape), whole((256, 256)),
            part(r_two), part(l_two), part(r_two),
        ],
        out_specs=pl.BlockSpec((pairs, group, 2, WIDTH, WIDTH), lambda g: (0, g, 0, 0, 0)),
        out_shape=jax.ShapeDtypeStruct((pairs, bins, 2, WIDTH, WIDTH), jnp.bfloat16),
        scratch_shapes=[
            pltpu.VMEM((pairs, 2 * WIDTH, WIDTH), jnp.bfloat16),
            pltpu.VMEM((pairs, 2 * WIDTH, WIDTH), jnp.bfloat16),
            pltpu.VMEM((group * 128, 2 * whole_tiles(r_count) + whole_tiles(l_count) + WIDTH), jnp.bfloat16),
        ],
        compiler_params=pltpu.CompilerParams(vmem_limit_bytes=VMEM),
        cost_estimate=pl.CostEstimate(
            flops=2 * peers * rows * 2 * WIDTH * (4 * pairs * WIDTH + 2 * r_two + l_two),
            bytes_accessed=2 * (peers * rows * (2 * r_two + l_two) + pairs * bins * 2 * WIDTH * WIDTH),
            transcendentals=0,
        ),
    )(info, where, regroup, xr, xl, zr)


def shards(samples, valid_counts, channel_mask, block_pairs):
    segs, channels, samples_len = samples.shape
    block_count = valid_counts.shape[0]
    planes = lax.axis_size("blk")
    peers = lax.axis_size("seg") * lax.axis_size("freq")
    pairs = block_pairs.shape[0]
    bins = samples_len // 2

    table, regroup = lax.optimization_barrier(
        (jnp.asarray(transform_table(bins, samples_len)), jnp.asarray(regroup_matrix()))
    )
    within = jnp.arange(WIDTH, dtype=jnp.int32)[None, :] < valid_counts[:, None]
    valid = (within & (channel_mask.reshape(block_count, WIDTH) == 1)).astype(jnp.int32)
    lines = jnp.pad(block_pairs.T, ((0, block_count - 2), (0, WIDTH - pairs)))
    own = jnp.concatenate([valid, lines], 0)
    others = [
        lax.ppermute(own, "blk", [(i, (i - shift) % planes) for i in range(planes)]) for shift in range(1, planes)
    ]
    me = lax.axis_index("blk").astype(jnp.int32).reshape(1, 1)
    place, where, info, branch = plan(me, own, others, block_count, pairs)
    place_row = place.reshape(1, channels)
    scale = 1.0 / math.sqrt(peers * segs)

    def with_sizes(r_count, l_count):
        def run(samples, table, regroup, place_row, where, info):
            own_r = spectra_chunk(samples, table, place_row, HB * WIDTH, whole_tiles(r_count) - r_count, r_count, peers, r_count < 320)
            xr = lax.all_to_all(own_r, ("seg", "freq"), split_axis=0, concat_axis=0, tiled=True)
            own_l = spectra_chunk(samples, table, place_row, channels, whole_tiles(r_count), l_count, peers, False)
            xr, own_l = lax.optimization_barrier((xr, own_l))
            zr = lax.ppermute(xr, "blk", [(i, i - 1) for i in range(1, planes)])
            info = after(info, zr)
            xl = lax.all_to_all(own_l, ("seg", "freq"), split_axis=0, concat_axis=0, tiled=True)
            return stacked_products(xr, xl, zr, info, where, regroup, pairs, scale)

        return run

    return lax.switch(
        branch[0, 0],
        [with_sizes(r, l) for r, l in SIZES],
        samples, table, regroup, place_row, where, info,
    )


def solution(mesh):
    placed = (P(("seg", "freq"), "blk", None), P("blk"), P("blk"), P("blk", None))
    return jax.shard_map(
        shards,
        mesh=mesh,
        in_specs=placed,
        out_specs=P("blk", ("seg", "freq"), None, None, None),
        check_vma=False,
    )
```
